32 devices in a mesh: grp: 2 (over x), ka: 16 (over z, y, core).
Axes of the slice: x: 2, y: 2, z: 4, core: 2. Of those that a mesh axis runs over, the one named last changes fastest.
Arguments:
- left_amps: bfloat16 [32, 6656, 624], P(('grp', 'ka')), parts along dimension 0, may hold values from -6 to 6
- right_amps: bfloat16 [32, 3, 6656, 104], P('grp', None, 'ka'), parts along dimension 0, may hold values from -0.0390625 to 0.0390625
- allowed: int32 [32, 3], P('grp'), parts along dimension 0, may hold values 0 or 1
Outputs:
- density_vv: float32 [32, 64896], P(('grp', 'ka')), parts along dimension 0
- density_oo: float32 [32, 384], P(('grp', 'ka')), parts along dimension 0
The draws below stay inside these ranges and needn't reach their ends.
There are 2 independent parts, one for each index of `grp`. The reference program is written for one: setup_inputs(seed, part) draws one part's arguments, and reference() takes and returns one part's arrays. A program takes and returns all parts, laid end to end along the dimension named above; each array names one. Nothing has to cross between parts.
All inputs are finite; a program needn't handle non-finite values.
Results may differ from the reference program's by a relative error of at most 0.0003.
Values may be sent and summed in bfloat16 or wider, within the bound.
A program may use at most 128 MiB of HBM per device.

```python
import jax
import jax.numpy as jnp
from jax import lax

NO = 8
NV = 104
NL = 6
W = 3
K = 16
M = 6656


def place_ends(drawn, rng, smallest, high):
    longest = drawn.shape.index(max(drawn.shape))
    spots = []
    for shift in (0, 1):
        where = [jax.random.randint(jax.random.fold_in(rng, axis), (), 0, length) for axis, length in enumerate(drawn.shape)]
        where[longest] = (where[longest] + shift) % drawn.shape[longest]
        spots.append(tuple(where))
    return drawn.at[spots[0]].set(smallest).at[spots[1]].set(high)


def steps_of(key, extent, pieces, low, top_value):
    def one(position, parts):
        steps = jax.random.uniform(jax.random.fold_in(jax.random.fold_in(key, 6), position), (parts,), jnp.float32, low / len(pieces), top_value / len(pieces))
        return jnp.repeat(jnp.exp(steps), extent[position] // parts).reshape((-1,) + (1,) * (len(extent) - position - 1))

    factor_of = one(*pieces[0])
    for cut in pieces[1:]:
        factor_of = factor_of * one(*cut)
    return factor_of


def bell_draw(own_key, extent, spread, bound, split=(), kind=jnp.bfloat16):
    result = jax.random.normal(own_key, extent, jnp.float32) * spread
    if len(split) > 0:
        result = steps_of(own_key, extent, split, -0.22, 0.18) * result
    return jnp.clip(result, min=-bound, max=bound).astype(kind)


def setup_inputs(seed: int = 0, part: int = 0) -> dict:
    key_of = jax.random.split(jax.random.key(seed), 4)
    part_keys = jax.random.split(jax.random.fold_in(key_of[3], part), 4)
    left_amps = bell_draw(part_keys[0], (K, M, NL * NV), 1.0, 6.0, ((0, 16),))
    right_amps = bell_draw(part_keys[1], (K, W, M, NV), (W * NO * NO * NV) ** -0.5, 0.0390625, ((2, 16),))
    allowed = place_ends((jax.random.randint(part_keys[2], (K, W), 0, 4) < 3).astype(jnp.int32), jax.random.fold_in(part_keys[2], 1), 0, 1)
    return {"left_amps": left_amps, "right_amps": right_amps, "allowed": allowed}


def contract(left_block, right_block):
    square = jnp.dot(left_block.T, right_block, precision=lax.Precision.HIGHEST, preferred_element_type=jnp.float32)
    left_view = left_block.reshape(NO, NO * NV, NL, NV)
    right_view = right_block.reshape(NO, NO * NV, NV)
    occupied = -jnp.einsum("ipra,jpa->rij", left_view, right_view, precision=lax.Precision.HIGHEST)
    return square.reshape(-1), occupied.reshape(-1)


def reference(left_amps, right_amps, allowed):
    count_points = left_amps.shape[0]
    window_count = right_amps.shape[1]
    middle = window_count // 2

    def per_point(point):
        total_vv = jnp.zeros((NL * NV * NV,), jnp.float32)
        total_oo = jnp.zeros((NL * NO * NO,), jnp.float32)
        right_rows = lax.dynamic_index_in_dim(right_amps, point, 0, keepdims=False)
        permits = lax.dynamic_index_in_dim(allowed, point, 0, keepdims=False)
        for window in range(window_count):
            source = ((point + (window - middle)) % count_points).astype(jnp.int32)
            left_block = lax.dynamic_index_in_dim(left_amps, source, 0, keepdims=False).astype(jnp.float32)
            right_block = right_rows[window].astype(jnp.float32)
            permit = permits[window].astype(jnp.float32)
            square, occupied = contract(left_block, right_block)
            total_vv = total_vv + permit * square
            total_oo = total_oo + permit * occupied
        return total_vv, total_oo

    density_vv, density_oo = lax.map(per_point, jnp.arange(count_points, dtype=jnp.int32))
    return density_vv, density_oo
```

```python
import jax
import jax.numpy as jnp
from jax import lax
from jax.sharding import PartitionSpec as P

NO = 8
NV = 104
NL = 6


def shifted(block, by):
    length = lax.axis_size("ka")
    return lax.ppermute(block, "ka", [(i, (i + by) % length) for i in range(length)])


def local(left_amps, right_amps, allowed):
    windows = right_amps.shape[1]
    middle = windows // 2
    count = lax.axis_size("ka")
    position = lax.axis_index("ka")
    lined = jnp.stack(
        [jnp.roll(right_amps[:, w], w - middle, axis=0) for w in range(windows)], axis=1
    )
    relaid = lax.all_to_all(lined, "ka", split_axis=0, concat_axis=2, tiled=True)[0]
    left = left_amps[0]
    right = relaid.transpose(1, 0, 2).reshape(-1, windows * NV)
    square = lax.dot_general(
        left, right, (((0,), (0,)), ((), ())), preferred_element_type=jnp.float32
    ).reshape(NL * NV, windows, NV)
    occupied = -jnp.einsum(
        "ipra,wjpa->wrij",
        left.reshape(NO, NO * NV, NL, NV),
        relaid.reshape(windows, NO, NO * NV, NV),
        preferred_element_type=jnp.float32,
    )
    total_vv = 0.0
    total_oo = 0.0
    for w in range(windows):
        point = (position - (w - middle)) % count
        factor = allowed[point, w].astype(jnp.float32)
        vv = (square[:, w] * factor).reshape(-1)
        oo = (occupied[w] * factor).reshape(-1)
        if w != middle:
            vv = shifted(vv, middle - w)
            oo = shifted(oo, middle - w)
        total_vv = total_vv + vv
        total_oo = total_oo + oo
    return (total_vv[None], total_oo[None])


def solution(mesh):
    in_specs = (P(("grp", "ka"), None, None), P("grp", None, "ka", None), P("grp", None))
    out_specs = (P(("grp", "ka"), None), P(("grp", "ka"), None))
    return jax.shard_map(local, mesh=mesh, in_specs=in_specs, out_specs=out_specs, check_vma=False)
```

```python
import functools

import jax
import jax.numpy as jnp
from jax import lax
from jax.experimental import pallas as pl
from jax.experimental.pallas import tpu as pltpu
from jax.sharding import PartitionSpec as P

NO = 8
NV = 104
NL = 6
W = 3
LANES = 128
GROUP = 8
SPARE = (LANES - NV) // GROUP
PIECES = NV // GROUP
BLOCKS = -(-PIECES // SPARE)
MESH = pl.DeviceIdType.MESH
LEFT_COLUMNS = NL * NV
COLUMN_TILES = -(-LEFT_COLUMNS // LANES)
F32 = jnp.float32


def tail_rows(rows):
    return rows // (BLOCKS + 1) // 16 * 16


def lane_index(rows):
    return lax.broadcasted_iota(jnp.int32, (rows, LANES), 1)


def pack(source, packed, rows):
    tail = tail_rows(rows)
    head = rows - tail
    lane = lane_index(tail)
    rest = jnp.concatenate(
        [source[head:rows, :].astype(F32), jnp.zeros((tail, LANES - NV), F32)], axis=1
    )
    for block in range(BLOCKS):
        row = block * tail
        out = jnp.concatenate(
            [source[row:row + tail, :].astype(F32), jnp.zeros((tail, LANES - NV), F32)], axis=1
        )
        for group in range(SPARE):
            piece = group * BLOCKS + block
            if piece < PIECES:
                place = NV + GROUP * group
                moved = pltpu.roll(rest, (place - GROUP * piece) % LANES, 1)
                out = jnp.where((lane >= place) & (lane < place + GROUP), moved, out)
        packed[row:row + tail, :] = out.astype(jnp.bfloat16)
    done = BLOCKS * tail
    if done < head:
        packed[done:head, :] = jnp.concatenate(
            [source[done:head, :], jnp.zeros((head - done, LANES - NV), jnp.bfloat16)], axis=1
        )


def unpack(packed, plain, rows):
    tail = tail_rows(rows)
    head = rows - tail
    lane = lane_index(tail)
    plain[0:head, :] = packed[0:head, :]
    rest = jnp.zeros((tail, LANES), F32)
    for block in range(BLOCKS):
        value = packed[block * tail:(block + 1) * tail, :].astype(F32)
        for group in range(SPARE):
            piece = group * BLOCKS + block
            if piece < PIECES:
                start = GROUP * piece
                moved = pltpu.roll(value, (start - NV - GROUP * group) % LANES, 1)
                rest = jnp.where((lane >= start) & (lane < start + GROUP), moved, rest)
    plain[head:rows, :] = rest.astype(jnp.bfloat16)


def kernel(count, rows, left_hbm, right_hbm, allowed, vv_out, oo_out, left, right, packed, landed,
           plain, tiled, vv, oo, leave, arrive, local_sem, send_sem, recv_sem, give_sem, take_sem):
    me = lax.axis_index("ka")
    half_count = count // 2

    def partner(n):
        step = lax.rem(n, 2) * ((n + 1) // 2) + (1 - lax.rem(n, 2)) * (half_count + n // 2)
        place, bit = 0, 1
        while bit < count:
            place = place + lax.rem(lax.rem(me // bit, 2) + lax.rem(step // bit, 2), 2) * bit
            bit *= 2
        return place

    def send(w, target):
        return pltpu.make_async_remote_copy(
            src_ref=packed.at[w, target], dst_ref=landed.at[w, me],
            send_sem=send_sem.at[w, target], recv_sem=recv_sem.at[w, me],
            device_id={"ka": target}, device_id_type=MESH)

    def receive(w, source):
        return pltpu.make_async_remote_copy(
            src_ref=packed.at[w, source], dst_ref=landed.at[w, source],
            send_sem=send_sem.at[w, source], recv_sem=recv_sem.at[w, source],
            device_id={"ka": source}, device_id_type=MESH)

    order = (0, 2, 1)
    fetch = {w: pltpu.make_async_copy(right_hbm.at[:, w], right.at[w], local_sem.at[w]) for w in order}
    for w in order:
        fetch[w].start()
    fetch_left = pltpu.make_async_copy(left_hbm, left, local_sem.at[W])
    fetch_left.start()

    barrier = pltpu.get_barrier_semaphore()

    @pl.loop(0, count - 1)
    def _(n):
        pl.semaphore_signal(barrier, inc=1, device_id={"ka": partner(n)}, device_id_type=MESH)

    vv[...] = jnp.zeros_like(vv)
    oo[...] = jnp.zeros_like(oo)

    for place, w in enumerate(order):
        fetch[w].wait()
        if place == 0:
            pl.semaphore_wait(barrier, count - 1)

        @pl.loop(0, count - 1)
        def _(n):
            target = partner(n)
            point = lax.rem(target + count - (w - 1), count)
            pack(right.at[w, point], packed.at[w, target], rows)
            send(w, target).start()

    fetch_left.wait()

    def multiply(windows, source):
        here = left.at[pl.ds(pl.multiple_of(source * rows, 16), rows), :]
        for w in windows:
            vv[w] += lax.dot_general(here[...], plain[w], (((0,), (0,)), ((), ())),
                                     preferred_element_type=F32)
        for w in windows:
            @pl.loop(0, rows // 16)
            def _(chunk):
                at = pl.ds(pl.multiple_of(chunk * 16, 16), 16)
                value = plain[w, at, :].astype(F32)
                lane = lane_index(16)
                for tile in range(COLUMN_TILES):
                    skip = tile * LANES % NV
                    first = pltpu.roll(value, (-skip) % LANES, 1) if skip else value
                    then = pltpu.roll(value, (NV - skip) % LANES, 1)
                    tiled[w, at, tile * LANES:(tile + 1) * LANES] = jnp.where(
                        lane < NV - skip, first, then)

        share = NO * rows // (NO * NV)
        per_index = NO * NV // rows
        outer = source // per_index
        start = lax.rem(source, per_index) * rows

        @pl.loop(0, NO)
        def _(i):
            def step(chunk, sums):
                at = pl.ds(pl.multiple_of(i * (NO * NV) + start + chunk * 16, 16), 16)
                value = left[at, :].astype(F32)
                near = pl.ds(pl.multiple_of(chunk * 16, 16), 16)
                out = []
                for w, total in zip(windows, sums):
                    product = value * tiled[w, near, :LEFT_COLUMNS]
                    out.append(total + product[:8] + product[8:])
                return tuple(out)

            sums = lax.fori_loop(0, rows // 16, step,
                                 tuple(jnp.zeros((8, LEFT_COLUMNS), F32) for _ in windows), unroll=2)
            for w, total in zip(windows, sums):
                oo[w, i, pl.ds(outer, 1), :] += jnp.sum(total, axis=0, keepdims=True)

    def phase(windows):
        for w in windows:
            plain[w] = jnp.concatenate(
                [right[w, lax.rem(me + count - (w - 1), count)],
                 jnp.zeros((rows, LANES - NV), jnp.bfloat16)], axis=1)
        multiply(windows, me)

        @pl.loop(0, count - 1)
        def _(n):
            source = partner(n)
            for w in windows:
                receive(w, source).wait_recv()
                unpack(landed.at[w, source], plain.at[w], rows)
            multiply(windows, source)

    column = lax.broadcasted_iota(jnp.int32, (8, LEFT_COLUMNS), 1)
    vector = lax.broadcasted_iota(jnp.int32, (8, LEFT_COLUMNS), 0)
    pick = ((column >= vector * NV) & (column < (vector + 1) * NV)).astype(F32)

    def occupied(w):
        return -lax.dot_general(pick, oo[w].reshape(NO * NO, LEFT_COLUMNS), (((1,), (1,)), ((), ())),
                                precision=lax.Precision.HIGHEST, preferred_element_type=F32)

    phase((0, 2))
    moves = []
    for slot, (w, target) in enumerate(((0, lax.rem(me + 1, count)), (2, lax.rem(me + count - 1, count)))):
        leave[slot, 0:LEFT_COLUMNS, :] = vv[w]
        leave[slot, LEFT_COLUMNS:LEFT_COLUMNS + 8, 0:NO * NO] = occupied(w)
        leave[slot, LEFT_COLUMNS:LEFT_COLUMNS + 8, NO * NO:] = jnp.zeros((8, LANES - NO * NO), F32)
        move = pltpu.make_async_remote_copy(
            src_ref=leave.at[slot], dst_ref=arrive.at[slot], send_sem=give_sem.at[slot],
            recv_sem=take_sem.at[slot], device_id={"ka": target}, device_id_type=MESH)
        move.start()
        moves.append(move)
    phase((1,))
    for move in moves:
        move.wait()
    factor = [allowed[me, w].astype(F32) for w in range(W)]
    vv_out[...] = (factor[1] * vv[1] + factor[0] * arrive[0, 0:LEFT_COLUMNS, :]
                   + factor[2] * arrive[1, 0:LEFT_COLUMNS, :])[:, :NV]
    oo_out[...] = (factor[1] * occupied(1)
                   + factor[0] * arrive[0, LEFT_COLUMNS:LEFT_COLUMNS + 8, 0:NO * NO]
                   + factor[2] * arrive[1, LEFT_COLUMNS:LEFT_COLUMNS + 8, 0:NO * NO])
    for w in order:
        @pl.loop(0, count - 1)
        def _(n):
            send(w, partner(n)).wait_send()


def kernel_local(left_amps, right_amps, allowed):
    count, _, rows, _ = right_amps.shape
    all_rows = left_amps.shape[1]
    vv, oo = pl.pallas_call(
        functools.partial(kernel, count, rows),
        out_shape=(jax.ShapeDtypeStruct((LEFT_COLUMNS, NV), F32),
                   jax.ShapeDtypeStruct((8, NO * NO), F32)),
        in_specs=[pl.BlockSpec(memory_space=pl.ANY), pl.BlockSpec(memory_space=pl.ANY),
                  pl.BlockSpec(memory_space=pltpu.SMEM)],
        out_specs=[pl.BlockSpec(memory_space=pltpu.VMEM)] * 2,
        scratch_shapes=[
            pltpu.VMEM((all_rows, LEFT_COLUMNS), jnp.bfloat16),
            pltpu.VMEM((W, count, rows, NV), jnp.bfloat16),
            pltpu.VMEM((W, count, rows - tail_rows(rows), LANES), jnp.bfloat16),
            pltpu.VMEM((W, count, rows - tail_rows(rows), LANES), jnp.bfloat16),
            pltpu.VMEM((W, rows, LANES), jnp.bfloat16),
            pltpu.VMEM((W, rows, COLUMN_TILES * LANES), F32),
            pltpu.VMEM((W, LEFT_COLUMNS, LANES), F32),
            pltpu.VMEM((W, NO, NO, LEFT_COLUMNS), F32),
            pltpu.VMEM((2, LEFT_COLUMNS + 8, LANES), F32),
            pltpu.VMEM((2, LEFT_COLUMNS + 8, LANES), F32),
            pltpu.SemaphoreType.DMA((W + 1,)),
            pltpu.SemaphoreType.DMA((W, count)),
            pltpu.SemaphoreType.DMA((W, count)),
            pltpu.SemaphoreType.DMA((2,)),
            pltpu.SemaphoreType.DMA((2,)),
        ],
        compiler_params=pltpu.CompilerParams(
            collective_id=0, has_side_effects=True, vmem_limit_bytes=56 * 1024 * 1024),
        cost_estimate=pl.CostEstimate(
            flops=2 * W * all_rows * LEFT_COLUMNS * NV, transcendentals=0,
            bytes_accessed=2 * all_rows * (LEFT_COLUMNS + W * NV)),
    )(left_amps[0], right_amps, allowed)
    return (vv.reshape(1, -1), oo[:NL].reshape(1, -1))


def shifted(block, by):
    length = lax.axis_size("ka")
    return lax.ppermute(block, "ka", [(i, (i + by) % length) for i in range(length)])


def plain_local(left_amps, right_amps, allowed):
    windows = right_amps.shape[1]
    middle = windows // 2
    count = lax.axis_size("ka")
    position = lax.axis_index("ka")
    lined = jnp.stack(
        [jnp.roll(right_amps[:, w], w - middle, axis=0) for w in range(windows)], axis=1
    )
    relaid = lax.all_to_all(lined, "ka", split_axis=0, concat_axis=2, tiled=True)[0]
    left = left_amps[0]
    right = relaid.transpose(1, 0, 2).reshape(-1, windows * NV)
    square = lax.dot_general(
        left, right, (((0,), (0,)), ((), ())), preferred_element_type=jnp.float32
    ).reshape(NL * NV, windows, NV)
    occupied = -jnp.einsum(
        "ipra,wjpa->wrij",
        left.reshape(NO, NO * NV, NL, NV),
        relaid.reshape(windows, NO, NO * NV, NV),
        preferred_element_type=jnp.float32,
    )
    total_vv = 0.0
    total_oo = 0.0
    for w in range(windows):
        point = (position - (w - middle)) % count
        factor = allowed[point, w].astype(jnp.float32)
        vv = (square[:, w] * factor).reshape(-1)
        oo = (occupied[w] * factor).reshape(-1)
        if w != middle:
            vv = shifted(vv, middle - w)
            oo = shifted(oo, middle - w)
        total_vv = total_vv + vv
        total_oo = total_oo + oo
    return (total_vv[None], total_oo[None])


def local(left_amps, right_amps, allowed):
    count, _, rows, _ = right_amps.shape
    if rows % 16 == 0 and (NO * NV) % rows == 0 and count & (count - 1) == 0:
        return kernel_local(left_amps, right_amps, allowed)
    return plain_local(left_amps, right_amps, allowed)


def solution(mesh):
    in_specs = (P(("grp", "ka"), None, None), P("grp", None, "ka", None), P("grp", None))
    out_specs = (P(("grp", "ka"), None), P(("grp", "ka"), None))
    return jax.shard_map(local, mesh=mesh, in_specs=in_specs, out_specs=out_specs, check_vma=False)
```

```python
import functools

import jax
import jax.numpy as jnp
from jax import lax
from jax.experimental import pallas as pl
from jax.experimental.pallas import tpu as pltpu
from jax.sharding import PartitionSpec as P

NO = 8
NV = 104
NL = 6
W = 3
LANES = 128
GROUP = 8
SPARE = (LANES - NV) // GROUP
PIECES = NV // GROUP
BLOCKS = -(-PIECES // SPARE)
MESH = pl.DeviceIdType.MESH
LEFT_COLUMNS = NL * NV
PAIR = 2
F32 = jnp.float32


def tail_rows(rows):
    return rows // (BLOCKS + 1) // 16 * 16


def lane_index(rows):
    return lax.broadcasted_iota(jnp.int32, (rows, LANES), 1)


def pack(source, packed, rows):
    tail = tail_rows(rows)
    head = rows - tail
    lane = lane_index(tail)
    rest = jnp.concatenate(
        [source[head:rows, :].astype(F32), jnp.zeros((tail, LANES - NV), F32)], axis=1
    )
    for block in range(BLOCKS):
        row = block * tail
        out = jnp.concatenate(
            [source[row:row + tail, :].astype(F32), jnp.zeros((tail, LANES - NV), F32)], axis=1
        )
        for group in range(SPARE):
            piece = group * BLOCKS + block
            if piece < PIECES:
                place = NV + GROUP * group
                moved = pltpu.roll(rest, (place - GROUP * piece) % LANES, 1)
                out = jnp.where((lane >= place) & (lane < place + GROUP), moved, out)
        packed[row:row + tail, :] = out.astype(jnp.bfloat16)
    done = BLOCKS * tail
    if done < head:
        packed[done:head, :] = jnp.concatenate(
            [source[done:head, :], jnp.zeros((head - done, LANES - NV), jnp.bfloat16)], axis=1
        )


def unpack(packed, plain, first, lanes, rows):
    tail = tail_rows(rows)
    head = rows - tail
    lane = lane_index(tail)
    plain[pl.ds(first, head), lanes] = packed[0:head, :]
    rest = jnp.zeros((tail, LANES), F32)
    for block in range(BLOCKS):
        value = packed[block * tail:(block + 1) * tail, :].astype(F32)
        for group in range(SPARE):
            piece = group * BLOCKS + block
            if piece < PIECES:
                start = GROUP * piece
                moved = pltpu.roll(value, (start - NV - GROUP * group) % LANES, 1)
                rest = jnp.where((lane >= start) & (lane < start + GROUP), moved, rest)
    plain[pl.ds(pl.multiple_of(first + head, 16), tail), lanes] = rest.astype(jnp.bfloat16)


def kernel(count, rows, left_hbm, right_hbm, allowed, vv_out, oo_out, left, right, packed, landed,
           plain, vv, oo, leave, arrive, local_sem, send_sem, recv_sem, give_sem, take_sem):
    me = lax.axis_index("ka")
    chips = count // PAIR
    half = chips // 2
    sibling = me + 1 - 2 * lax.rem(me, PAIR)
    span = NO * NV
    edge = (-span) % LANES

    def other_chip(n):
        step = lax.rem(n, 2) * ((n + 1) // 2) + (1 - lax.rem(n, 2)) * (half + n // 2)
        chip, place, bit = me // PAIR, 0, 1
        while bit < chips:
            place = place + lax.rem(lax.rem(chip // bit, 2) + lax.rem(step // bit, 2), 2) * bit
            bit *= 2
        return place

    def send(target):
        return pltpu.make_async_remote_copy(
            src_ref=packed.at[target], dst_ref=landed.at[me],
            send_sem=send_sem.at[target], recv_sem=recv_sem.at[me],
            device_id={"ka": target}, device_id_type=MESH)

    def receive(source):
        return pltpu.make_async_remote_copy(
            src_ref=packed.at[source], dst_ref=landed.at[source],
            send_sem=send_sem.at[source], recv_sem=recv_sem.at[source],
            device_id={"ka": source}, device_id_type=MESH)

    fetch = pltpu.make_async_copy(right_hbm, right, local_sem.at[0])
    fetch.start()
    fetch_left = pltpu.make_async_copy(left_hbm, left, local_sem.at[1])
    fetch_left.start()

    barrier = pltpu.get_barrier_semaphore()

    @pl.loop(1, count)
    def _(n):
        pl.semaphore_signal(barrier, inc=1, device_id={"ka": lax.rem(me + n, count)},
                            device_id_type=MESH)

    plain[...] = jnp.zeros_like(plain)
    vv[...] = jnp.zeros_like(vv)
    oo[...] = jnp.zeros_like(oo)
    fetch.wait()

    def prepare(target):
        for w in range(W):
            point = lax.rem(target + count - (w - W // 2), count)
            pack(right.at[point, w], packed.at[target, w], rows)

    for n in range(chips - 1):
        for core in range(PAIR):
            target = other_chip(n) * PAIR + core
            prepare(target)
            if n == 0 and core == 0:
                pl.semaphore_wait(barrier, count - 1)
            send(target).start()
        if n == 0:
            prepare(sibling)
            send(sibling).start()
    fetch_left.wait()

    row = lax.broadcasted_iota(jnp.int32, (LEFT_COLUMNS, LANES), 0)
    column = lax.broadcasted_iota(jnp.int32, (LEFT_COLUMNS, LANES), 1)
    same = lax.rem(row, NV) == column

    def product(i, outer):
        odd = lax.rem(i, 2)
        at = pl.ds(pl.multiple_of(i * span - odd * edge, LANES), span + edge)
        near = pl.ds(pl.multiple_of((1 - odd) * edge, 16), span + edge)
        square = jnp.dot(left[:, at], plain[near, :], preferred_element_type=F32)
        for w in range(W):
            kept = jnp.where(same, square[:, w * LANES:(w + 1) * LANES], 0.0)
            for r in range(NL):
                oo[w, outer * NO + i, r:r + 1, :] = jnp.sum(
                    kept[r * NV:(r + 1) * NV], axis=0, keepdims=True)
        return square

    def multiply(outer):
        vv[...] += product(outer, outer)

        @pl.loop(1, NO)
        def _(n):
            product(lax.rem(outer + n, NO), outer)

    for w in range(W):
        point = lax.rem(me + count - (w - W // 2), count)
        plain[pl.ds(pl.multiple_of(edge + lax.rem(me, PAIR) * rows, 16), rows),
              w * LANES:w * LANES + NV] = right[point, w]
    receive(sibling).wait_recv()
    for w in range(W):
        unpack(landed.at[sibling, w], plain, pl.multiple_of(edge + lax.rem(sibling, PAIR) * rows, 16),
               slice(w * LANES, (w + 1) * LANES), rows)
    multiply(me // PAIR)

    @pl.loop(0, chips - 1)
    def _(n):
        chip = other_chip(n)
        for core in range(PAIR):
            source = chip * PAIR + core
            receive(source).wait_recv()
            for w in range(W):
                unpack(landed.at[source, w], plain, edge + core * rows,
                       slice(w * LANES, (w + 1) * LANES), rows)
        multiply(chip)

    def occupied(w):
        return -jnp.sum(oo[w], axis=2)

    moves = []
    for slot, (w, target) in enumerate(((0, lax.rem(me + 1, count)), (2, lax.rem(me + count - 1, count)))):
        leave[slot, 0:LEFT_COLUMNS, :] = vv[:, w * LANES:(w + 1) * LANES]
        leave[slot, LEFT_COLUMNS:, :] = jnp.concatenate(
            [occupied(w), jnp.zeros((NO * NO, LANES - 8), F32)], axis=1)
        move = pltpu.make_async_remote_copy(
            src_ref=leave.at[slot], dst_ref=arrive.at[slot], send_sem=give_sem.at[slot],
            recv_sem=take_sem.at[slot], device_id={"ka": target}, device_id_type=MESH)
        move.start()
        moves.append(move)
    factor = [allowed[w, me].astype(F32) for w in range(W)]
    centre = factor[1] * occupied(1)

    @pl.loop(1, count)
    def _(n):
        send(lax.rem(me + n, count)).wait_send()

    for move in moves:
        move.wait()
    vv_out[...] = (factor[1] * vv[:, LANES:2 * LANES] + factor[0] * arrive[0, 0:LEFT_COLUMNS, :]
                   + factor[2] * arrive[1, 0:LEFT_COLUMNS, :])[:, :NV]
    oo_out[...] = (centre + factor[0] * arrive[0, LEFT_COLUMNS:, 0:8]
                   + factor[2] * arrive[1, LEFT_COLUMNS:, 0:8])


def kernel_local(left_amps, right_amps, allowed):
    count, _, rows, _ = right_amps.shape
    all_rows = left_amps.shape[1]
    head = rows - tail_rows(rows)
    extent = NO * NV + 2 * ((-NO * NV) % LANES)
    vv, oo = pl.pallas_call(
        functools.partial(kernel, count, rows),
        out_shape=(jax.ShapeDtypeStruct((LEFT_COLUMNS, NV), F32),
                   jax.ShapeDtypeStruct((NO * NO, 8), F32)),
        in_specs=[pl.BlockSpec(memory_space=pl.ANY), pl.BlockSpec(memory_space=pl.ANY),
                  pl.BlockSpec(memory_space=pltpu.SMEM)],
        out_specs=[pl.BlockSpec(memory_space=pltpu.VMEM)] * 2,
        scratch_shapes=[
            pltpu.VMEM((LEFT_COLUMNS, all_rows), jnp.bfloat16),
            pltpu.VMEM((count, W, rows, NV), jnp.bfloat16),
            pltpu.VMEM((count, W, head, LANES), jnp.bfloat16),
            pltpu.VMEM((count, W, head, LANES), jnp.bfloat16),
            pltpu.VMEM((extent, W * LANES), jnp.bfloat16),
            pltpu.VMEM((LEFT_COLUMNS, W * LANES), F32),
            pltpu.VMEM((W, NO * NO, 8, LANES), F32),
            pltpu.VMEM((2, LEFT_COLUMNS + NO * NO, LANES), F32),
            pltpu.VMEM((2, LEFT_COLUMNS + NO * NO, LANES), F32),
            pltpu.SemaphoreType.DMA((2,)),
            pltpu.SemaphoreType.DMA((count,)),
            pltpu.SemaphoreType.DMA((count,)),
            pltpu.SemaphoreType.DMA((2,)),
            pltpu.SemaphoreType.DMA((2,)),
        ],
        compiler_params=pltpu.CompilerParams(
            collective_id=0, has_side_effects=True, vmem_limit_bytes=56 * 1024 * 1024),
        cost_estimate=pl.CostEstimate(
            flops=2 * W * all_rows * LEFT_COLUMNS * NV * NO, transcendentals=0,
            bytes_accessed=2 * all_rows * (LEFT_COLUMNS + W * NV)),
    )(left_amps[0].T, right_amps, allowed.T)
    oo = oo[:, :NL].reshape(NO, NO, NL).transpose(2, 1, 0)
    return (vv.reshape(1, -1), oo.reshape(1, -1))


def shifted(block, by):
    length = lax.axis_size("ka")
    return lax.ppermute(block, "ka", [(i, (i + by) % length) for i in range(length)])


def plain_local(left_amps, right_amps, allowed):
    windows = right_amps.shape[1]
    middle = windows // 2
    count = lax.axis_size("ka")
    position = lax.axis_index("ka")
    lined = jnp.stack(
        [jnp.roll(right_amps[:, w], w - middle, axis=0) for w in range(windows)], axis=1
    )
    relaid = lax.all_to_all(lined, "ka", split_axis=0, concat_axis=2, tiled=True)[0]
    left = left_amps[0]
    right = relaid.transpose(1, 0, 2).reshape(-1, windows * NV)
    square = lax.dot_general(
        left, right, (((0,), (0,)), ((), ())), preferred_element_type=jnp.float32
    ).reshape(NL * NV, windows, NV)
    occupied = -jnp.einsum(
        "ipra,wjpa->wrij",
        left.reshape(NO, NO * NV, NL, NV),
        relaid.reshape(windows, NO, NO * NV, NV),
        preferred_element_type=jnp.float32,
    )
    total_vv = 0.0
    total_oo = 0.0
    for w in range(windows):
        point = (position - (w - middle)) % count
        factor = allowed[point, w].astype(jnp.float32)
        vv = (square[:, w] * factor).reshape(-1)
        oo = (occupied[w] * factor).reshape(-1)
        if w != middle:
            vv = shifted(vv, middle - w)
            oo = shifted(oo, middle - w)
        total_vv = total_vv + vv
        total_oo = total_oo + oo
    return (total_vv[None], total_oo[None])


def local(left_amps, right_amps, allowed):
    count, _, rows, _ = right_amps.shape
    if rows % 16 == 0 and NO * NV == PAIR * rows and count == PAIR * NO:
        return kernel_local(left_amps, right_amps, allowed)
    return plain_local(left_amps, right_amps, allowed)


def solution(mesh):
    in_specs = (P(("grp", "ka"), None, None), P("grp", None, "ka", None), P("grp", None))
    out_specs = (P(("grp", "ka"), None), P(("grp", "ka"), None))
    return jax.shard_map(local, mesh=mesh, in_specs=in_specs, out_specs=out_specs, check_vma=False)
```
